32 devices in a mesh: seq: 16 (over z, y, x), head: 2 (over core).
Axes of the slice: x: 2, y: 2, z: 4, core: 2. Of those that a mesh axis runs over, the one named last changes fastest.
Arguments:
- queries: bfloat16 [6144, 8192], P('seq', 'head'), may hold values from -6 to 6
- keys: bfloat16 [6144, 8192], P('seq', 'head'), may hold values from -6 to 6
- values: bfloat16 [6144, 8192], P('seq', 'head'), may hold values from -6 to 6
- norm_gain: float32 [8192], P('head'), may hold values from 0.25 to 1.75
- out_weight: bfloat16 [8192, 6144], P(None, 'head'), may hold values from -0.0625 to 0.0625
Outputs:
- layer_out: bfloat16 [6144, 6144], P('seq', 'head')
The draws below stay inside these ranges and needn't reach their ends.
All inputs are finite; a program needn't handle non-finite values.
Results may differ from the reference program's by a relative error of at most 0.0058.
Values may be sent and summed in bfloat16 or wider, within the bound.
A program may use at most 192 MiB of HBM per device.

```python
import jax
import jax.numpy as jnp
from jax import lax

D = 6144
HEADS = 64
HEAD_DIM = 128
TOK_DEV = 384
HD = 8192
TOKENS = 6144


def steps_of(stream_key, extent, shards, smallest, top_value):
    factor_of, own = 1.0, jax.random.fold_in(stream_key, 6)
    for dim, parts in shards:
        draws = jnp.exp(jax.random.uniform(jax.random.fold_in(own, dim), (parts,), jnp.float32, smallest / len(shards), top_value / len(shards)))
        factor_of = factor_of * jnp.repeat(draws, extent[dim] // parts).reshape([-1 if axis == dim else 1 for axis in range(len(extent))])
    return factor_of


def gaussian(own_key, extent, deviation, bound, split=(), kind=jnp.bfloat16):
    factor_of = steps_of(own_key, extent, split, -0.22, 0.18) if split else 1.0
    entries = jax.random.normal(own_key, extent, jnp.float32) * deviation * factor_of
    return jnp.minimum(jnp.maximum(entries, -bound), bound).astype(kind)


def setup_inputs(seed: int = 0) -> dict:
    streams_of = jax.random.split(jax.random.key(seed), 6)
    return {
        "queries": gaussian(streams_of[0], (TOKENS, HD), 1.0, 6.0, ((0, 16), (1, 2))),
        "keys": gaussian(streams_of[1], (TOKENS, HD), 1.0, 6.0, ((0, 16), (1, 2))),
        "values": gaussian(streams_of[2], (TOKENS, HD), 1.0, 6.0, ((0, 16), (1, 2))),
        "norm_gain": jnp.clip(1.0 + 0.15 * jax.random.normal(streams_of[3], (HD,), jnp.float32), 0.25, 1.75),
        "out_weight": gaussian(streams_of[4], (HD, D), HD ** -0.5, 0.0625, ((1, 2),)),
    }


def reference(queries, keys, values, norm_gain, out_weight):
    blocks = TOKENS // TOK_DEV
    qa = jax.nn.silu(queries.astype(jnp.float32)).astype(jnp.bfloat16)
    ka = jax.nn.silu(keys.astype(jnp.float32)).astype(jnp.bfloat16)
    qa = lax.optimization_barrier(qa)
    ka = lax.optimization_barrier(ka)
    qa = qa.reshape(blocks, TOK_DEV, HEADS, HEAD_DIM)
    ka = ka.reshape(blocks, TOK_DEV, HEADS, HEAD_DIM)
    vv = values.reshape(blocks, TOK_DEV, HEADS, HEAD_DIM)
    gain = norm_gain.reshape(HEADS, HEAD_DIM)
    causal = jnp.arange(TOK_DEV)[:, None] >= jnp.arange(TOK_DEV)[None, :]
    high = lax.Precision.HIGHEST

    def step(state, inputs):
        qb, kb, vb = inputs
        qf = qb.astype(jnp.float32)
        kf = kb.astype(jnp.float32)
        vf = vb.astype(jnp.float32)
        inter = jnp.einsum('thd,hde->the', qf, state, precision=high)
        scores = jnp.einsum('thd,shd->hts', qf, kf, precision=high)
        scores = jnp.where(causal[None], scores, 0.0).astype(jnp.bfloat16)
        scores = lax.optimization_barrier(scores).astype(jnp.float32)
        intra = jnp.einsum('hts,she->the', scores, vf, precision=high)
        attn = inter + intra
        mean_sq = lax.optimization_barrier(jnp.mean(attn * attn, axis=-1, keepdims=True))
        normed = (attn * lax.rsqrt(mean_sq + 1e-06) * gain[None]).astype(jnp.bfloat16)
        state = state + jnp.einsum('thd,the->hde', kf, vf, precision=high)
        return (state, normed)
    start = jnp.zeros((HEADS, HEAD_DIM, HEAD_DIM), jnp.float32)
    final_state, normed = lax.scan(step, start, (qa, ka, vv))
    normed = normed.reshape(TOKENS, HD)
    return jnp.dot(normed, out_weight, preferred_element_type=jnp.float32).astype(jnp.bfloat16)
```

```python
import functools

import jax
import jax.numpy as jnp
from jax import lax
from jax.experimental import pallas as pl
from jax.experimental.pallas import tpu as pltpu
from jax.sharding import PartitionSpec as P

HEAD_DIM = 128
MEMBERS = 4
MESH = pl.DeviceIdType.MESH
F32, BF16 = jnp.float32, jnp.bfloat16


def silu(x):
    half = 0.5 * x.astype(F32)
    return (half * (1.0 + jnp.tanh(half))).astype(BF16)


def loop(count, body):
    def step(i, carry):
        body(i)
        return carry

    lax.fori_loop(0, count, step, 0)


def kernel(
    n, m, q_hbm, k_hbm, v_hbm, gain_ref, w_hbm, out_hbm,
    qb, kb, vb, intra, stage, held, chain_in, chain_out, ret_out, ret_in, normed, acc, outb, wb,
    load_sem, w_sem, s1_send, s1_recv, ch_send, ch_recv, rt_send, rt_recv, hd_send, hd_recv, out_sem,
):
    parts, members, rows, width = qb.shape
    per = width // HEAD_DIM
    groups = n // members
    slots = wb.shape[0]
    columns = acc.shape[1]
    tile = 512 if columns % 512 == 0 else columns
    tiles = columns // tile
    own_heads = parts * per
    local = members * own_heads

    seq, head = lax.axis_index("seq"), lax.axis_index("head")
    group, member = lax.div(seq, members), lax.rem(seq, members)

    def mate(d):
        return lax.rem(member + d, members)

    def seq_of(i):
        return {"seq": group * members + i}

    def load(which, hbm, buf, p, j):
        at = pl.multiple_of((j * own_heads + p * per) * HEAD_DIM, HEAD_DIM)
        return pltpu.make_async_copy(
            hbm.at[:, pl.ds(at, width)], buf.at[p, j], load_sem.at[which, p, j]
        )

    def weights(s, j):
        p, r = lax.div(s, m), lax.rem(s, m)
        source = lax.rem(head + r, m)
        at = pl.multiple_of((source * local + j * own_heads + p * per) * HEAD_DIM, HEAD_DIM)
        slot = lax.rem(s, slots)
        return pltpu.make_async_copy(
            w_hbm.at[pl.ds(at, width), :], wb.at[slot, pl.ds(j * width, width), :], w_sem.at[slot, j]
        )

    def to_owner(p, j):
        return pltpu.make_async_remote_copy(
            src_ref=stage.at[p, j], dst_ref=held.at[p, member],
            send_sem=s1_send.at[p, j], recv_sem=s1_recv.at[p, member],
            device_id=seq_of(j), device_id_type=MESH,
        )

    def from_mate(p, i):
        return pltpu.make_async_remote_copy(
            src_ref=stage.at[p, i], dst_ref=held.at[p, i],
            send_sem=s1_send.at[p, i], recv_sem=s1_recv.at[p, i],
            device_id=seq_of(i), device_id_type=MESH,
        )

    def chain(p):
        return pltpu.make_async_remote_copy(
            src_ref=chain_out.at[p], dst_ref=chain_in.at[p],
            send_sem=ch_send.at[p], recv_sem=ch_recv.at[p],
            device_id={"seq": lax.rem(seq + members, n)}, device_id_type=MESH,
        )

    def give_back(p, i):
        return pltpu.make_async_remote_copy(
            src_ref=ret_out.at[p, i], dst_ref=ret_in.at[p, member],
            send_sem=rt_send.at[p, i], recv_sem=rt_recv.at[p, member],
            device_id=seq_of(i), device_id_type=MESH,
        )

    def get_back(p, j):
        return pltpu.make_async_remote_copy(
            src_ref=ret_out.at[p, j], dst_ref=ret_in.at[p, j],
            send_sem=rt_send.at[p, j], recv_sem=rt_recv.at[p, j],
            device_id=seq_of(j), device_id_type=MESH,
        )

    def to_head(p, r):
        return pltpu.make_async_remote_copy(
            src_ref=normed.at[p, 0], dst_ref=normed.at[p, m - r],
            send_sem=hd_send.at[p, r], recv_sem=hd_recv.at[p, m - r],
            device_id={"head": lax.rem(head + r, m)}, device_id_type=MESH,
        )

    def from_head(p, r):
        return pltpu.make_async_remote_copy(
            src_ref=normed.at[p, 0], dst_ref=normed.at[p, r],
            send_sem=hd_send.at[p, r], recv_sem=hd_recv.at[p, r],
            device_id={"head": lax.rem(head + r, m)}, device_id_type=MESH,
        )

    def write(t):
        cols = pl.ds(pl.multiple_of(t * tile, tile), tile)
        return pltpu.make_async_copy(outb.at[:, cols], out_hbm.at[:, cols], out_sem.at[t])

    def start_loads(p):
        def both(j):
            load(0, k_hbm, kb, p, j).start()
            load(1, v_hbm, vb, p, j).start()

        loop(members, both)

    loop(parts, start_loads)
    loop(parts, lambda p: loop(members, lambda j: load(2, q_hbm, qb, p, j).start()))
    loop(slots, lambda s: loop(members, lambda j: weights(s, j).start()))

    barrier = pltpu.get_barrier_semaphore()
    for d in range(1, members):
        pl.semaphore_signal(barrier, inc=1, device_id=seq_of(mate(d)), device_id_type=MESH)
    for r in range(1, m):
        pl.semaphore_signal(
            barrier, inc=1, device_id={"head": lax.rem(head + r, m)}, device_id_type=MESH
        )

    @pl.when(group > 0)
    def _():
        pl.semaphore_signal(
            barrier, inc=1, device_id={"seq": lax.rem(seq - members + n, n)}, device_id_type=MESH
        )

    @pl.when(group < groups - 1)
    def _():
        pl.semaphore_signal(
            barrier, inc=1, device_id={"seq": lax.rem(seq + members, n)}, device_id_type=MESH
        )

    beside = jnp.where(group > 0, 1, 0) + jnp.where(group < groups - 1, 1, 0)
    pl.semaphore_wait(barrier, members - 1 + m - 1 + beside)

    def states(p):
        def one(d):
            j = mate(d + 1)
            load(0, k_hbm, kb, p, j).wait()
            load(1, v_hbm, vb, p, j).wait()
            ka = silu(kb[p, j])
            kb[p, j] = ka
            both = lax.dot_general(
                ka, vb[p, j], (((0,), (0,)), ((), ())), preferred_element_type=F32
            )
            diagonal = [
                both[c * HEAD_DIM : (c + 1) * HEAD_DIM, c * HEAD_DIM : (c + 1) * HEAD_DIM].astype(BF16)
                for c in range(per)
            ]

            @pl.when(j != member)
            def _():
                for c in range(per):
                    stage[p, j, c] = diagonal[c]
                to_owner(p, j).start()

            @pl.when(j == member)
            def _():
                for c in range(per):
                    held[p, member, c] = diagonal[c]

        loop(members, one)

    def combine(p):
        for d in range(1, members):
            from_mate(p, mate(d)).wait_recv()

        @pl.when(group > 0)
        def _():
            chain(p).wait_recv()

        @pl.when(group == 0)
        def _():
            chain_in[p] = jnp.zeros(chain_in.shape[1:], F32)

        @pl.when(group < groups - 1)
        def _():
            total = chain_in[p]
            for i in range(members):
                total = total + held[p, i].astype(F32)
            chain_out[p] = total
            chain(p).start()

        before = chain_in[p]
        for i in range(members):
            rounded = before.astype(BF16)

            @pl.when(member != i)
            def _():
                ret_out[p, i] = rounded
                give_back(p, i).start()

            @pl.when(member == i)
            def _():
                ret_in[p, i] = rounded

            if i < members - 1:
                before = before + held[p, i].astype(F32)

    block = 128 if rows % 128 == 0 else rows

    def inside(p):
        at_or_before = (
            lax.broadcasted_iota(jnp.int32, (block, block), 0)
            >= lax.broadcasted_iota(jnp.int32, (block, block), 1)
        )

        def one(j):
            load(2, q_hbm, qb, p, j).wait()
            qb[p, j] = silu(qb[p, j])
            for c in range(per):
                lanes = slice(c * HEAD_DIM, (c + 1) * HEAD_DIM)
                for b in range(rows // block):
                    tokens = slice(b * block, (b + 1) * block)
                    upto = slice(0, (b + 1) * block)
                    qa = qb[p, j, tokens, lanes]
                    scores = lax.dot_general(
                        qa, kb[p, j, upto, lanes], (((1,), (1,)), ((), ())),
                        preferred_element_type=F32,
                    )
                    last = jnp.where(at_or_before, scores[:, b * block :], 0.0).astype(BF16)
                    if b:
                        last = jnp.concatenate(
                            [scores[:, : b * block].astype(BF16), last], axis=1
                        )
                    intra[p, j, tokens, lanes] = jnp.dot(
                        last, vb[p, j, upto, lanes], preferred_element_type=F32
                    )

        loop(members, one)

    def project(s, a):
        slot = lax.rem(s, slots)
        loop(members, lambda j: weights(s, j).wait())

        def one(t):
            cols = pl.ds(pl.multiple_of(t * tile, tile), tile)
            acc[:, cols] += jnp.dot(a[...], wb[slot, :, cols], preferred_element_type=F32)

        loop(tiles, one)

        @pl.when(s + slots < parts * m)
        def _():
            loop(members, lambda j: weights(s + slots, j).start())

    def finish(p):
        for d in range(1, members):
            get_back(p, mate(d)).wait_recv()

        def one(j):
            for c in range(per):
                lanes = slice(c * HEAD_DIM, (c + 1) * HEAD_DIM)
                inter = jnp.dot(qb[p, j, :, lanes], ret_in[p, j, c], preferred_element_type=F32)
                attn = inter + intra[p, j, :, lanes]
                mean_sq = jnp.mean(attn * attn, axis=-1, keepdims=True)
                value = attn * lax.rsqrt(mean_sq + 1e-06) * gain_ref[j, p, :, lanes]
                at = pl.multiple_of(j * width + c * HEAD_DIM, HEAD_DIM)
                normed[p, 0, :, pl.ds(at, HEAD_DIM)] = value.astype(BF16)

        loop(members, one)
        loop(m - 1, lambda r: to_head(p, r + 1).start())
        project(p * m, normed.at[p, 0])

        def other(r):
            from_head(p, r + 1).wait_recv()
            project(p * m + r + 1, normed.at[p, r + 1])

        loop(m - 1, other)

    loop(parts, states)
    acc[...] = jnp.zeros(acc.shape, F32)

    def slot_step(t):
        u = t - group

        @pl.when((u >= 0) & (u < parts))
        def _():
            combine(u)

        @pl.when(t < parts)
        def _():
            inside(t)

        @pl.when(t >= groups)
        def _():
            finish(t - groups)

    loop(parts + groups, slot_step)

    def emit(t):
        cols = pl.ds(pl.multiple_of(t * tile, tile), tile)
        outb[:, cols] = acc[:, cols].astype(BF16)
        write(t).start()

    loop(tiles, emit)

    def sent(p):
        for d in range(1, members):
            to_owner(p, mate(d)).wait_send()
            give_back(p, mate(d)).wait_send()

        @pl.when(group < groups - 1)
        def _():
            chain(p).wait_send()

        loop(m - 1, lambda r: to_head(p, r + 1).wait_send())

    loop(parts, sent)
    loop(tiles, lambda t: write(t).wait())


def shards(n, m, queries, keys, values, norm_gain, out_weight):
    rows, wide = queries.shape
    columns = out_weight.shape[1]
    heads = wide // HEAD_DIM
    own = heads // MEMBERS
    per = 2 if own % 2 == 0 else 1
    parts = own // per
    width = per * HEAD_DIM
    slots = min(4, parts * m)
    tile = 512 if columns % 512 == 0 else columns
    gain = norm_gain.reshape(MEMBERS, parts, 1, width)
    square = (per, HEAD_DIM, HEAD_DIM)
    grid = (parts, MEMBERS)
    dma = pltpu.SemaphoreType.DMA
    anywhere = pl.BlockSpec(memory_space=pl.ANY)
    return pl.pallas_call(
        functools.partial(kernel, n, m),
        out_shape=jax.ShapeDtypeStruct((rows, columns), BF16),
        in_specs=[anywhere] * 3 + [pl.BlockSpec(memory_space=pltpu.VMEM), anywhere],
        out_specs=anywhere,
        scratch_shapes=[
            pltpu.VMEM(grid + (rows, width), BF16),
            pltpu.VMEM(grid + (rows, width), BF16),
            pltpu.VMEM(grid + (rows, width), BF16),
            pltpu.VMEM(grid + (rows, width), F32),
            pltpu.VMEM(grid + square, BF16),
            pltpu.VMEM(grid + square, BF16),
            pltpu.VMEM((parts,) + square, F32),
            pltpu.VMEM((parts,) + square, F32),
            pltpu.VMEM(grid + square, BF16),
            pltpu.VMEM(grid + square, BF16),
            pltpu.VMEM((parts, m, rows, MEMBERS * width), BF16),
            pltpu.VMEM((rows, columns), F32),
            pltpu.VMEM((rows, columns), BF16),
            pltpu.VMEM((slots, MEMBERS * width, columns), BF16),
            dma((3,) + grid),
            dma((slots, MEMBERS)),
            dma(grid), dma(grid),
            dma((parts,)), dma((parts,)),
            dma(grid), dma(grid),
            dma((parts, m)), dma((parts, m)),
            dma((columns // tile,)),
        ],
        compiler_params=pltpu.CompilerParams(
            collective_id=0, has_side_effects=True, vmem_limit_bytes=63 * 1024 * 1024
        ),
        cost_estimate=pl.CostEstimate(
            flops=2 * rows * wide * m * columns, bytes_accessed=2 * wide * m * columns,
            transcendentals=2 * rows * wide,
        ),
    )(queries, keys, values, gain, out_weight)


def solution(mesh):
    n, m = mesh.shape["seq"], mesh.shape["head"]
    in_specs = (P("seq", "head"), P("seq", "head"), P("seq", "head"), P("head"), P(None, "head"))
    return jax.shard_map(
        functools.partial(shards, n, m), mesh=mesh, in_specs=in_specs,
        out_specs=P("seq", "head"), check_vma=False,
    )
```

```python
import functools

import jax
import jax.numpy as jnp
from jax import lax
from jax.experimental import pallas as pl
from jax.experimental.pallas import tpu as pltpu
from jax.sharding import PartitionSpec as P

HEAD_DIM = 128
MEMBERS = 4
MESH = pl.DeviceIdType.MESH
F32, BF16 = jnp.float32, jnp.bfloat16


def silu(x):
    half = 0.5 * x.astype(F32)
    return (half * (1.0 + jnp.tanh(half))).astype(BF16)


def loop(count, body, unroll=False):
    def step(i, carry):
        body(i)
        return carry

    lax.fori_loop(0, count, step, 0, unroll=unroll)


def kernel(
    n, m, q_hbm, k_hbm, v_hbm, gain_ref, w_hbm, out_hbm,
    qb, kb, vb, intra, stage, held, chain_in, chain_out, ret_out, ret_in, normed, acc, outb, wb,
    load_sem, w_sem, s1_send, s1_recv, ch_send, ch_recv, rt_send, rt_recv, hd_send, hd_recv, out_sem,
):
    parts, members, rows, width = qb.shape
    per = width // HEAD_DIM
    groups = n // members
    slots = wb.shape[0]
    columns = acc.shape[1]
    tile = 1536 if columns % 1536 == 0 else columns
    tiles = columns // tile
    own_heads = parts * per
    local = members * own_heads

    seq, head = lax.axis_index("seq"), lax.axis_index("head")
    group, member = lax.div(seq, members), lax.rem(seq, members)

    def mate(d):
        return lax.rem(member + d, members)

    def seq_of(i):
        return {"seq": group * members + i}

    def load(which, hbm, buf, p, j):
        at = pl.multiple_of((j * own_heads + p * per) * HEAD_DIM, HEAD_DIM)
        return pltpu.make_async_copy(
            hbm.at[:, pl.ds(at, width)], buf.at[p, j], load_sem.at[which, p, j]
        )

    def weights(s, j):
        p, r = lax.div(s, m), lax.rem(s, m)
        source = lax.rem(head + r, m)
        at = pl.multiple_of((source * local + j * own_heads + p * per) * HEAD_DIM, HEAD_DIM)
        slot = lax.rem(s, slots)
        return pltpu.make_async_copy(
            w_hbm.at[pl.ds(at, width), :], wb.at[slot, pl.ds(j * width, width), :], w_sem.at[slot, j]
        )

    def to_owner(p, j):
        return pltpu.make_async_remote_copy(
            src_ref=stage.at[p, j], dst_ref=held.at[p, member],
            send_sem=s1_send.at[p, j], recv_sem=s1_recv.at[p, member],
            device_id=seq_of(j), device_id_type=MESH,
        )

    def from_mate(p, i):
        return pltpu.make_async_remote_copy(
            src_ref=stage.at[p, i], dst_ref=held.at[p, i],
            send_sem=s1_send.at[p, i], recv_sem=s1_recv.at[p, i],
            device_id=seq_of(i), device_id_type=MESH,
        )

    def chain(p):
        return pltpu.make_async_remote_copy(
            src_ref=chain_out.at[p], dst_ref=chain_in.at[p],
            send_sem=ch_send.at[p], recv_sem=ch_recv.at[p],
            device_id={"seq": lax.rem(seq + members, n)}, device_id_type=MESH,
        )

    def give_back(p, i):
        return pltpu.make_async_remote_copy(
            src_ref=ret_out.at[p, i], dst_ref=ret_in.at[p, member],
            send_sem=rt_send.at[p, i], recv_sem=rt_recv.at[p, member],
            device_id=seq_of(i), device_id_type=MESH,
        )

    def get_back(p, j):
        return pltpu.make_async_remote_copy(
            src_ref=ret_out.at[p, j], dst_ref=ret_in.at[p, j],
            send_sem=rt_send.at[p, j], recv_sem=rt_recv.at[p, j],
            device_id=seq_of(j), device_id_type=MESH,
        )

    def to_head(p, r):
        return pltpu.make_async_remote_copy(
            src_ref=normed.at[p, 0], dst_ref=normed.at[p, m - r],
            send_sem=hd_send.at[p, r], recv_sem=hd_recv.at[p, m - r],
            device_id={"head": lax.rem(head + r, m)}, device_id_type=MESH,
        )

    def from_head(p, r):
        return pltpu.make_async_remote_copy(
            src_ref=normed.at[p, 0], dst_ref=normed.at[p, r],
            send_sem=hd_send.at[p, r], recv_sem=hd_recv.at[p, r],
            device_id={"head": lax.rem(head + r, m)}, device_id_type=MESH,
        )

    def write(t):
        cols = pl.ds(pl.multiple_of(t * tile, tile), tile)
        return pltpu.make_async_copy(outb.at[:, cols], out_hbm.at[:, cols], out_sem.at[t])

    def start_loads(p):
        def both(j):
            load(0, k_hbm, kb, p, j).start()
            load(1, v_hbm, vb, p, j).start()

        loop(members, both)

    loop(parts, start_loads)
    loop(parts, lambda p: loop(members, lambda j: load(2, q_hbm, qb, p, j).start()))
    loop(slots, lambda s: loop(members, lambda j: weights(s, j).start()))

    barrier = pltpu.get_barrier_semaphore()
    for d in range(1, members):
        pl.semaphore_signal(barrier, inc=1, device_id=seq_of(mate(d)), device_id_type=MESH)
    for r in range(1, m):
        pl.semaphore_signal(
            barrier, inc=1, device_id={"head": lax.rem(head + r, m)}, device_id_type=MESH
        )

    @pl.when(group > 0)
    def _():
        pl.semaphore_signal(
            barrier, inc=1, device_id={"seq": lax.rem(seq - members + n, n)}, device_id_type=MESH
        )

    @pl.when(group < groups - 1)
    def _():
        pl.semaphore_signal(
            barrier, inc=1, device_id={"seq": lax.rem(seq + members, n)}, device_id_type=MESH
        )

    beside = jnp.where(group > 0, 1, 0) + jnp.where(group < groups - 1, 1, 0)
    pl.semaphore_wait(barrier, members - 1 + m - 1 + beside)

    def states(p):
        def one(d):
            j = mate(d + 1)
            load(0, k_hbm, kb, p, j).wait()
            load(1, v_hbm, vb, p, j).wait()
            ka = silu(kb[p, j])
            kb[p, j] = ka
            both = lax.dot_general(
                ka, vb[p, j], (((0,), (0,)), ((), ())), preferred_element_type=F32
            )
            diagonal = [
                both[c * HEAD_DIM : (c + 1) * HEAD_DIM, c * HEAD_DIM : (c + 1) * HEAD_DIM].astype(BF16)
                for c in range(per)
            ]

            @pl.when(j != member)
            def _():
                for c in range(per):
                    stage[p, j, c] = diagonal[c]
                to_owner(p, j).start()

            @pl.when(j == member)
            def _():
                for c in range(per):
                    held[p, member, c] = diagonal[c]

        loop(members, one)

    def combine(p):
        for d in range(1, members):
            from_mate(p, mate(d)).wait_recv()

        @pl.when(group > 0)
        def _():
            chain(p).wait_recv()

        @pl.when(group == 0)
        def _():
            chain_in[p] = jnp.zeros(chain_in.shape[1:], F32)

        @pl.when(group < groups - 1)
        def _():
            total = chain_in[p]
            for i in range(members):
                total = total + held[p, i].astype(F32)
            chain_out[p] = total
            chain(p).start()

        before = chain_in[p]
        for i in range(members):
            rounded = before.astype(BF16)

            @pl.when(member != i)
            def _():
                ret_out[p, i] = rounded
                give_back(p, i).start()

            @pl.when(member == i)
            def _():
                ret_in[p, i] = rounded

            if i < members - 1:
                before = before + held[p, i].astype(F32)

    block = rows

    def inside(p):
        at_or_before = (
            lax.broadcasted_iota(jnp.int32, (block, block), 0)
            >= lax.broadcasted_iota(jnp.int32, (block, block), 1)
        )

        def one(j):
            load(2, q_hbm, qb, p, j).wait()
            qa = silu(qb[p, j])
            qb[p, j] = qa
            for c in range(per):
                lanes = slice(c * HEAD_DIM, (c + 1) * HEAD_DIM)
                scores = lax.dot_general(
                    qa[:, lanes], kb[p, j, :, lanes], (((1,), (1,)), ((), ())),
                    preferred_element_type=F32,
                )
                scores = jnp.where(at_or_before, scores, 0.0).astype(BF16)
                intra[p, j, :, lanes] = jnp.dot(
                    scores, vb[p, j, :, lanes], preferred_element_type=F32
                )

        loop(members, one, True)

    def project(s, a):
        slot = lax.rem(s, slots)
        loop(members, lambda j: weights(s, j).wait())

        def one(t):
            cols = pl.ds(pl.multiple_of(t * tile, tile), tile)
            acc[:, cols] += jnp.dot(a[...], wb[slot, :, cols], preferred_element_type=F32)

        loop(tiles, one)

        @pl.when(s + slots < parts * m)
        def _():
            loop(members, lambda j: weights(s + slots, j).start())

    def finish(p):
        for d in range(1, members):
            get_back(p, mate(d)).wait_recv()

        def one(j):
            for c in range(per):
                lanes = slice(c * HEAD_DIM, (c + 1) * HEAD_DIM)
                inter = jnp.dot(qb[p, j, :, lanes], ret_in[p, j, c], preferred_element_type=F32)
                attn = inter + intra[p, j, :, lanes]
                mean_sq = jnp.mean(attn * attn, axis=-1, keepdims=True)
                value = attn * lax.rsqrt(mean_sq + 1e-06) * gain_ref[j, p, :, lanes]
                at = pl.multiple_of(j * width + c * HEAD_DIM, HEAD_DIM)
                normed[p, 0, :, pl.ds(at, HEAD_DIM)] = value.astype(BF16)

        loop(members, one, True)
        loop(m - 1, lambda r: to_head(p, r + 1).start())
        project(p * m, normed.at[p, 0])

        def other(r):
            from_head(p, r + 1).wait_recv()
            project(p * m + r + 1, normed.at[p, r + 1])

        loop(m - 1, other)

    loop(parts, states)
    acc[...] = jnp.zeros(acc.shape, F32)

    def slot_step(t):
        u = t - group

        @pl.when((u >= 0) & (u < parts))
        def _():
            combine(u)

        @pl.when(t < parts)
        def _():
            inside(t)

        @pl.when(t >= groups)
        def _():
            finish(t - groups)

    loop(parts + groups, slot_step)

    def emit(t):
        cols = pl.ds(pl.multiple_of(t * tile, tile), tile)
        outb[:, cols] = acc[:, cols].astype(BF16)
        write(t).start()

    loop(tiles, emit)

    def sent(p):
        for d in range(1, members):
            to_owner(p, mate(d)).wait_send()
            give_back(p, mate(d)).wait_send()

        @pl.when(group < groups - 1)
        def _():
            chain(p).wait_send()

        loop(m - 1, lambda r: to_head(p, r + 1).wait_send())

    loop(parts, sent)
    loop(tiles, lambda t: write(t).wait())


def shards(n, m, queries, keys, values, norm_gain, out_weight):
    rows, wide = queries.shape
    columns = out_weight.shape[1]
    heads = wide // HEAD_DIM
    own = heads // MEMBERS
    per = 2 if own % 2 == 0 else 1
    parts = own // per
    width = per * HEAD_DIM
    slots = min(4, parts * m)
    tile = 1536 if columns % 1536 == 0 else columns
    gain = norm_gain.reshape(MEMBERS, parts, 1, width)
    square = (per, HEAD_DIM, HEAD_DIM)
    grid = (parts, MEMBERS)
    dma = pltpu.SemaphoreType.DMA
    anywhere = pl.BlockSpec(memory_space=pl.ANY)
    return pl.pallas_call(
        functools.partial(kernel, n, m),
        out_shape=jax.ShapeDtypeStruct((rows, columns), BF16),
        in_specs=[anywhere] * 3 + [pl.BlockSpec(memory_space=pltpu.VMEM), anywhere],
        out_specs=anywhere,
        scratch_shapes=[
            pltpu.VMEM(grid + (rows, width), BF16),
            pltpu.VMEM(grid + (rows, width), BF16),
            pltpu.VMEM(grid + (rows, width), BF16),
            pltpu.VMEM(grid + (rows, width), F32),
            pltpu.VMEM(grid + square, BF16),
            pltpu.VMEM(grid + square, BF16),
            pltpu.VMEM((parts,) + square, F32),
            pltpu.VMEM((parts,) + square, F32),
            pltpu.VMEM(grid + square, BF16),
            pltpu.VMEM(grid + square, BF16),
            pltpu.VMEM((parts, m, rows, MEMBERS * width), BF16),
            pltpu.VMEM((rows, columns), F32),
            pltpu.VMEM((rows, columns), BF16),
            pltpu.VMEM((slots, MEMBERS * width, columns), BF16),
            dma((3,) + grid),
            dma((slots, MEMBERS)),
            dma(grid), dma(grid),
            dma((parts,)), dma((parts,)),
            dma(grid), dma(grid),
            dma((parts, m)), dma((parts, m)),
            dma((columns // tile,)),
        ],
        compiler_params=pltpu.CompilerParams(
            collective_id=0, has_side_effects=True, vmem_limit_bytes=63 * 1024 * 1024
        ),
        cost_estimate=pl.CostEstimate(
            flops=2 * rows * wide * m * columns, bytes_accessed=2 * wide * m * columns,
            transcendentals=2 * rows * wide,
        ),
    )(queries, keys, values, gain, out_weight)


def solution(mesh):
    n, m = mesh.shape["seq"], mesh.shape["head"]
    in_specs = (P("seq", "head"), P("seq", "head"), P("seq", "head"), P("head"), P(None, "head"))
    return jax.shard_map(
        functools.partial(shards, n, m), mesh=mesh, in_specs=in_specs,
        out_specs=P("seq", "head"), check_vma=False,
    )
```
